256 devices in a mesh: fsdp: 16 (over z, y_lo), dom: 16 (over y_hi, x, core).
Axes of the slice: x: 4, y: 4 (y_hi: 2, y_lo: 2; y = y_hi * 2 + y_lo), z: 8, core: 2. Of those that a mesh axis runs over, the one named last changes fastest.
Arguments:
- tokens: bfloat16 [65536, 8192], P(('fsdp', 'dom')), may hold values from -24 to 24
- key_grad: bfloat16 [65536, 512], P(('fsdp', 'dom')), may hold values from -6 to 6
- weight: bfloat16 [8192, 512], P('fsdp'), may hold values from -0.0625 to 0.0625
- master: float32 [8192, 512], P(('fsdp', 'dom')), may hold values from -0.0625 to 0.0625
- moment_one: float32 [8192, 512], P(('fsdp', 'dom')), may hold values from -3 to 3
- moment_two: float32 [8192, 512], P(('fsdp', 'dom')), may hold values from 0.1 to 4
- live: int32 [16, 16], replicated, may hold values from 0 to 1, as said below
- buddy: int32 [16], replicated, may hold values from 0 to 15, as said below
Outputs:
- keys: bfloat16 [65536, 512], P(('fsdp', 'dom'))
- input_grad: bfloat16 [65536, 8192], P(('fsdp', 'dom'))
- new_weight: bfloat16 [8192, 512], P('fsdp')
- new_master: float32 [8192, 512], P(('fsdp', 'dom'))
- new_one: float32 [8192, 512], P(('fsdp', 'dom'))
- new_two: float32 [8192, 512], P(('fsdp', 'dom'))
- held_copy: float32 [3, 8192, 512], P(None, ('fsdp', 'dom'))
The draws below stay inside these ranges and needn't reach their ends.
Inputs may be any that keep to these rules, and one draw needn't show every extreme that they name: `live`: every column (domain) has at least one 1. A permutation of the domains in a single cycle; no domain is its own buddy; some domain's buddy lies 16 / 2 domains further round.
All inputs are finite; a program needn't handle non-finite values.
Results may differ from the reference program's by a relative error of at most 0.005.
Values may be sent and summed in bfloat16 or wider, within the bound.
A program may use at most 128 MiB of HBM per device.

```python
import math
import jax
import jax.numpy as jnp
from jax import lax

D = 8192
TOK_DEV = 256
STEP = 100
KD = 512
FSDPS = 16
DOMS = 16
TOKENS = 65536


def draw_live(key, part):
    picks = jax.random.randint(jax.random.fold_in(key, 11), (FSDPS, DOMS), 0, 4)
    alive = (picks > 0).astype(jnp.int32)
    keeper = jax.random.randint(jax.random.fold_in(key, 12), (DOMS,), 0, FSDPS)
    forced = (jnp.arange(FSDPS)[:, None] == keeper[None, :]).astype(jnp.int32)
    return jnp.maximum(alive, forced).astype(jnp.int32)


def draw_buddy(key, part):
    shuffled = jax.random.permutation(jax.random.fold_in(key, 13), DOMS).astype(jnp.int32)
    first = jax.random.randint(jax.random.fold_in(key, 14), (), 0, DOMS).astype(jnp.int32)
    second = ((first + DOMS // 2) % DOMS).astype(jnp.int32)
    values = jnp.arange(DOMS, dtype=jnp.int32)
    place = jnp.zeros((DOMS,), jnp.int32).at[shuffled].set(values)
    score = jnp.where(values == first, -2, jnp.where(values == second, -1, place)).astype(jnp.int32)
    order = jnp.argsort(score, stable=True).astype(jnp.int32)
    return jnp.zeros((DOMS,), jnp.int32).at[order].set(jnp.roll(order, -1)).astype(jnp.int32)


def with_spikes(entries, own_key, source, target, shards_of, factor):
    def block_of(dim):
        return (jnp.arange(entries.shape[dim]) // (entries.shape[dim] // shards_of)).reshape((-1,) + (1,) * (entries.ndim - 1 - dim))

    one_side = jax.random.permutation(own_key, shards_of)[block_of(target)]
    far = (block_of(target) + shards_of // 2) % shards_of
    return jnp.where((block_of(source) == one_side) | (block_of(source) == far), factor * entries, entries)


def steps_of(rng, extent, split, low, top_value):
    def one(dim, parts):
        draws = jax.random.uniform(jax.random.fold_in(jax.random.fold_in(rng, 6), dim), (parts,), jnp.float32, low / len(split), top_value / len(split))
        return jnp.repeat(jnp.exp(draws), extent[dim] // parts).reshape((-1,) + (1,) * (len(extent) - dim - 1))

    loudness = one(*split[0])
    for cut in split[1:]:
        loudness = loudness * one(*cut)
    return loudness


def scatter_about(key, extent, width, bound, cuts=(), held_as=jnp.bfloat16):
    drawn = jax.random.normal(key, extent, jnp.float32) * width
    if len(cuts) > 0:
        drawn = steps_of(key, extent, cuts, -0.22, 0.18) * drawn
    return jnp.clip(drawn, min=-bound, max=bound).astype(held_as)


def gaussian_with(key, shape, spread, reach, split, heavy, kind=jnp.bfloat16):
    array = spread * jax.random.normal(key, shape, jnp.float32)
    if split:
        array = array * steps_of(key, shape, split, -0.22, 0.18)
    return jnp.clip(with_spikes(array, jax.random.fold_in(key, 3), *heavy), -reach, reach).astype(kind)


def setup_inputs(seed: int = 0) -> dict:
    key_of = jax.random.split(jax.random.key(seed), 9)
    tokens = gaussian_with(key_of[0], (TOKENS, D), 1.0, 24.0, ((0, 256),), (0, 1, 256, 6.0))
    key_grad = scatter_about(key_of[1], (TOKENS, KD), 1.0, 6.0, ((0, 256),))
    weight = scatter_about(key_of[2], (D, KD), D ** -0.5, 0.0625, ((0, 16),))
    master = scatter_about(key_of[3], (D, KD), D ** -0.5, 0.0625, ((0, 256),), jnp.float32)
    moment_one = scatter_about(key_of[4], (D, KD), 0.5, 3.0, ((0, 256),), jnp.float32)
    moment_two = jnp.clip(jnp.exp(math.log(4.0) - 3.6888794 * jax.random.uniform(key_of[5], (D, KD), jnp.float32) ** steps_of(key_of[5], (D, KD), ((0, 256),), -0.2, 0.2)), 0.1, 4.0)
    live = draw_live(jax.random.fold_in(key_of[8], 71), 0)
    buddy = draw_buddy(jax.random.fold_in(key_of[8], 71), 0)
    return dict(tokens=tokens, key_grad=key_grad, weight=weight, master=master, moment_one=moment_one, moment_two=moment_two, live=live, buddy=buddy)


def reference(tokens, key_grad, weight, master, moment_one, moment_two, live, buddy):
    devs = FSDPS * DOMS
    live_flat = live.reshape(-1).astype(jnp.float32)
    total = jnp.sum(live_flat)
    scales = live_flat * devs / (total * TOK_DEV)
    blocks = tokens.reshape(devs, TOK_DEV, D)
    cotans = key_grad.reshape(devs, TOK_DEV, KD)

    def step(carry, item):
        block, cotan, scale = item
        xf = block.astype(jnp.float32)
        rstd = lax.rsqrt(lax.optimization_barrier(jnp.mean(xf * xf, axis=1, keepdims=True)) + 1e-05)
        hat = xf * rstd
        normed = hat.astype(jnp.bfloat16)
        keys = jnp.dot(normed, weight, preferred_element_type=jnp.float32).astype(jnp.bfloat16)
        back = lax.dot_general(cotan, weight, (((1,), (1,)), ((), ())), preferred_element_type=jnp.float32)
        dx = (rstd * (back - hat * lax.optimization_barrier(jnp.mean(back * hat, axis=1, keepdims=True)))).astype(jnp.bfloat16)
        term = lax.dot_general(normed, cotan, (((0,), (0,)), ((), ())), preferred_element_type=jnp.float32)
        return (carry + term * scale, (keys, dx))
    grad, (keys, dx) = lax.scan(step, jnp.zeros((D, KD), jnp.float32), (blocks, cotans, scales))
    new_one = 0.9 * moment_one + 0.1 * grad
    new_two = 0.95 * moment_two + 0.05 * grad * grad
    first = 1.0 - 0.9 ** STEP
    second = 1.0 - 0.95 ** STEP
    update = new_one / first / (jnp.sqrt(new_two / second) + 1e-08)
    new_master = master - 0.002 * (update + 0.1 * master)
    new_weight = new_master.astype(jnp.bfloat16)
    inverse = jnp.zeros((DOMS,), jnp.int32).at[buddy].set(jnp.arange(DOMS, dtype=jnp.int32))
    rows = D // devs
    stacked = jnp.stack((new_master, new_one, new_two)).reshape(3, FSDPS, DOMS, rows, KD)
    held = jnp.take(stacked, inverse, axis=2).reshape(3, D, KD)
    return (keys.reshape(TOKENS, KD), dx.reshape(TOKENS, D), new_weight, new_master, new_one, new_two, held)
```

```python
import functools

import jax
import jax.numpy as jnp
from jax import lax
from jax.experimental import pallas as pl
from jax.experimental.pallas import tpu as pltpu
from jax.sharding import PartitionSpec as P

STEP = 100
F32 = jnp.float32
BF16 = jnp.bfloat16
MESH = pl.DeviceIdType.MESH
ORDER = (
    "send0", "prod0", "prod1", "pair0", "prod2", "pair1", "ag1", "prod3", "xb0", "pair2",
    "agy0", "comp0", "y0", "ag2", "agy1", "xb1", "pair3", "z0", "comp1", "y1", "ag3", "agy2",
    "xb2", "z1", "comp2", "y2", "ag4", "agy3", "xb3", "z2", "y3", "z3", "update", "agy4",
    "comp3", "comp4", "final", "spread",
)


def dot(a, b, ca, cb):
    return lax.dot_general(a, b, (((ca,), (cb,)), ((), ())), preferred_element_type=F32)


def kernel(
    tok_h, kg_h, w_h, ma_h, mo_h, mt_h, live_v, buddy_s,
    keys_h, ig_h, nw_h, nm_h, n1_h, n2_h, held_h,
    tok, kg, kgm, W, back, keysf, keysb, normed, rstd, dots, prod, R, XA, XB, YS, YR, ZS, ZR, Zown, GA,
    state, new, held,
    loc, pair_s, pair_r, xa_s, xa_r, xb_s, xb_r, ys_s, ys_r, zs_s, zs_r,
    az_s, az_r, ay_s, ay_r, sib_s, sib_r, ga_s, ga_r, gs_s, gs_r,
):
    f = lax.axis_index("fsdp")
    d = lax.axis_index("dom")
    z, ylo = lax.div(f, 2), lax.rem(f, 2)
    yhi, x, c = lax.div(d, 8), lax.rem(lax.div(d, 2), 4), lax.rem(d, 2)
    y = yhi * 2 + ylo
    o = 1 - c
    xp, xo, xm = lax.rem(x + 1, 4), lax.rem(x + 2, 4), lax.rem(x + 3, 4)

    def dev(x, y, z, c):
        return (z * 2 + lax.rem(y, 2), lax.div(y, 2) * 8 + x * 2 + c)

    def yat(j):
        return lax.rem(y + j, 4)

    def zat(j):
        return lax.rem(z + j, 8)

    sibling = dev(x, y, z, o)

    def local(i, src, dst):
        return pltpu.make_async_copy(src, dst, loc.at[i])

    def remote(src, dst, s, r, to):
        return pltpu.make_async_remote_copy(
            src_ref=src, dst_ref=dst, send_sem=s, recv_sem=r, device_id=to, device_id_type=MESH
        )

    loads = [
        local(0, w_h, W.at[f]),
        local(1, tok_h, tok),
        local(2, kg_h, kg),
        local(3, ma_h, state.at[0]),
        local(4, mo_h, state.at[1]),
        local(5, mt_h, state.at[2]),
    ]
    for copy in loads:
        copy.start()

    barrier = pltpu.get_barrier_semaphore()
    partners = [sibling]
    partners += [dev(lax.rem(x + i, 4), y, z, c) for i in (1, 2, 3)]
    partners += [dev(lax.rem(x + i, 4), yat(2), z, c) for i in (0, 1, 2, 3)]
    partners += [dev(x, yat(i), z, c) for i in (1, 3)]
    partners += [dev(x, y, zat(i), c) for i in range(1, 8)]
    for who in partners:
        pl.semaphore_signal(barrier, inc=1, device_id=who, device_id_type=MESH)
    pl.semaphore_wait(barrier, len(partners))

    def z_offset(k, core):
        one = 1 - 2 * core
        return -one * k if k <= 4 else one * (k - 4)

    def piece(k, core, other):
        zz = lax.rem(z + z_offset(k, core) + 8, 8)
        return zz * 2 + (1 - ylo if other else ylo)

    onward = dev(x, y, lax.rem(z + 1 - 2 * c + 8, 8), c)
    backward = dev(x, y, lax.rem(z - 1 + 2 * c + 8, 8), c)

    def az(k):
        to = onward if k < 5 else backward
        before = (k - 1) if k != 5 else 0
        src = W.at[piece(before, c, False), c]
        return remote(src, src, az_s.at[k - 1], az_r.at[k - 1], to)

    def az_in(k):
        src = W.at[piece(k, c, False), c]
        return remote(src, src, az_s.at[k - 1], az_r.at[k - 1], onward)

    def ay(k, side):
        src = W.at[piece(k, c, False), c, side]
        return remote(src, src, ay_s.at[k, side], ay_r.at[k, side], dev(x, yat(1 if side == 0 else 3), z, c))

    def ay_in(k, side):
        src = W.at[piece(k, c, True), c, side]
        return remote(src, src, ay_s.at[k, side], ay_r.at[k, side], dev(x, yat(1), z, c))

    def sib(k, other):
        src = W.at[piece(k, c, other), c]
        i = k + 8 * other
        return remote(src, src, sib_s.at[i], sib_r.at[i], sibling)

    def sib_in(k, other):
        src = W.at[piece(k, o, other), o]
        i = k + 8 * other
        return remote(src, src, sib_s.at[i], sib_r.at[i], sibling)

    sent = []

    def go(copy):
        copy.start()
        sent.append(copy)

    steps = {0: (0,), 1: (1, 5), 2: (2, 6), 3: (3, 7), 4: (4,)}

    def gather(s):
        for k in steps[s]:
            if s:
                az_in(k).wait_recv()
            if k == 0:
                go(az(1))
                go(az(5))
            elif k not in (4, 7):
                go(az(k + 1))
            go(ay(k, 0))
            go(ay(k, 1))
            if k:
                go(sib(k, False))

    def gather_y(s):
        for k in steps[s]:
            ay_in(k, 0).wait_recv()
            ay_in(k, 1).wait_recv()
            go(sib(k, True))

    def send0():
        loads[0].wait()
        gather(0)
        loads[1].wait()
        dots[...] = jnp.zeros_like(dots)

        @pl.loop(0, 16)
        def _(i):
            v = tok[:, pl.ds(pl.multiple_of(i * 512, 512), 512)].astype(F32)
            v = v * v
            dots[...] += (v[:, :128] + v[:, 128:256]) + (v[:, 256:384] + v[:, 384:])

        mean = jnp.sum(dots[...], axis=1, keepdims=True) * (1.0 / 8192)
        rstd[...] = jnp.broadcast_to(lax.rsqrt(mean + 1e-05), rstd.shape)
        dots[...] = jnp.zeros_like(dots)
        keysf[...] = jnp.zeros_like(keysf)
        live = live_v[...].astype(F32)
        rows = lax.broadcasted_iota(jnp.int32, live.shape, 0)
        cols = lax.broadcasted_iota(jnp.int32, live.shape, 1)
        alive = jnp.sum(jnp.where((rows == f) & (cols == d), live, 0.0))
        loads[2].wait()
        kgm[...] = (kg[...].astype(F32) * alive).astype(BF16)

    def wide(column):
        return jnp.concatenate([column] * 4, axis=1)

    def product(g):
        @pl.loop(0, 4)
        def _(fi):
            at = pl.ds(pl.multiple_of((g * 4 + fi) * 512, 512), 512)
            normed[:, at] = (tok[:, at].astype(F32) * wide(rstd[...])).astype(BF16)
            part = dot(normed[:, at], kgm[...], 0, 0).astype(BF16)
            for yy in range(2):
                for xx in range(4):
                    for cc in range(2):
                        row = yy * 256 + xx * 64 + cc * 32
                        prod[g, cc, xx, yy, fi] = part[row : row + 32]

        go(pair(g))

    def pair(g):
        return remote(prod.at[g, o], R.at[g], pair_s.at[g], pair_r.at[g], sibling)

    def xa(g, i):
        block, half, to = ((xo, 0, xp), (xp, 1, xp), (xo, 1, xm), (xm, 0, xm))[i]
        return remote(
            prod.at[g, c, block, half], XA.at[g, i], xa_s.at[g, i], xa_r.at[g, i], dev(to, y, z, c)
        )

    def xb(g, i):
        block = (xp, xm)[i]
        return remote(
            prod.at[g, c, block, i], XB.at[g, i], xb_s.at[g, i], xb_r.at[g, i], dev(block, y, z, c)
        )

    def ysend(g, j):
        return remote(
            YS.at[g, yat(j)], YR.at[g, j - 1], ys_s.at[g, j - 1], ys_r.at[g, j - 1], dev(x, yat(j), z, c)
        )

    def pair_sum(g):
        pair(g).wait_recv()

        @pl.loop(0, 8)
        def _(i):
            xx, yy = lax.div(i, 2), lax.rem(i, 2)
            for fi in range(4):
                prod[g, c, xx, yy, fi] = (
                    prod[g, c, xx, yy, fi].astype(F32) + R[g, xx, yy, fi].astype(F32)
                ).astype(BF16)

        for i in (0, 2, 1, 3):
            go(xa(g, i))

    def x_second(g):
        for i, block in ((0, xp), (1, xm)):
            xa(g, 2 * i).wait_recv()

            @pl.loop(0, 4)
            def _(fi):
                prod[g, c, block, i, fi] = (
                    prod[g, c, block, i, fi].astype(F32) + XA[g, 2 * i, fi].astype(F32)
                ).astype(BF16)

            go(xb(g, i))

    def y_stage(g):
        for half, i in ((0, 3), (1, 1)):
            xa(g, i).wait_recv()
            xb(g, half).wait_recv()

            @pl.loop(0, 4)
            def _(fi):
                total = prod[g, c, x, half, fi].astype(F32) + XA[g, i, fi].astype(F32)
                total = total + XB[g, half, fi].astype(F32)
                YS[g, half * 2 + lax.rem(fi, 2), lax.div(fi, 2)] = total.astype(BF16)

        for j in (2, 1, 3):
            go(ysend(g, j))

    def zsend(g, i):
        return remote(
            ZS.at[g, i], ZR.at[z], zs_s.at[g, i], zs_r.at[z], dev(x, y, 2 * g + i, c)
        )

    def z_stage(g):
        for j in (1, 2, 3):
            ysend(g, j).wait_recv()
        for i in range(2):
            total = YS[g, y, i].astype(F32)
            for j in range(3):
                total = total + YR[g, j, i].astype(F32)

            @pl.when(z == 2 * g + i)
            def _():
                Zown[...] = total

            @pl.when(z != 2 * g + i)
            def _():
                ZS[g, i] = total.astype(BF16)
                zsend(g, i).start()

    chip = lax.div(d, 2)
    others = [(i, j) for j in (0, 2) for i in range(4) if i or j]

    def spread_out(n):
        i, j = others[n]
        to = dev(lax.rem(x + i, 4), yat(j), z, c)
        return remote(GA.at[c, chip], GA.at[c, chip], ga_s.at[n], ga_r.at[n], to)

    def spread_in(n):
        i, j = others[n]
        xx, yy = lax.rem(x - i + 4, 4), yat(j)
        slot = GA.at[c, lax.div(yy, 2) * 4 + xx]
        return remote(slot, slot, ga_s.at[n], ga_r.at[n], sibling)

    def spread_pair():
        return remote(GA.at[c], GA.at[c], gs_s.at[0], gs_r.at[0], sibling)

    def spread_pair_in():
        return remote(GA.at[o], GA.at[o], gs_s.at[0], gs_r.at[0], sibling)

    outs = [
        local(0, new.at[0], nm_h),
        local(1, new.at[1], n1_h),
        local(2, new.at[2], n2_h),
        local(3, held, held_h),
        local(4, GA.at[0, :, 0], nw_h.at[:, 0]),
        local(5, GA.at[1, :, 0], nw_h.at[:, 1]),
        local(6, keysb, keys_h),
    ]

    def ig_out(i):
        at = pl.ds(pl.multiple_of(i * 1024, 1024), 1024)
        return pltpu.make_async_copy(tok.at[:, at], ig_h.at[:, at], loc.at[8 + i])

    def update():
        total = Zown[...]
        for j in range(1, 8):
            slot = zat(j)
            here = ZR.at[slot]
            remote(here, here, zs_s.at[0, 0], zs_r.at[slot], sibling).wait_recv()
            total = total + ZR[slot].astype(F32)
        live = live_v[...].astype(F32)
        grad = total * (256.0 / (jnp.sum(live) * 256.0))
        for copy in loads[3:]:
            copy.wait()
        one = 0.9 * state[1] + 0.1 * grad
        two = 0.95 * state[2] + 0.05 * grad * grad
        first = 1.0 - 0.9**STEP
        second = 1.0 - 0.95**STEP
        step = one / first / (jnp.sqrt(two / second) + 1e-08)
        master = state[0] - 0.002 * (step + 0.1 * state[0])
        for i, v in enumerate((master, one, two)):
            new[i] = v
            GA[c, chip, i] = v.astype(BF16)
        for n in range(7):
            go(spread_out(n))
        for copy in outs[:3]:
            copy.start()

    def spread():
        for n in range(7):
            spread_in(n).wait_recv()
        go(spread_pair())
        spread_pair_in().wait_recv()
        outs[4].start()
        outs[5].start()
        src = jnp.int32(0)
        for s in range(16):
            src = jnp.where(buddy_s[s] == d, s, src)
        held[...] = GA[lax.rem(src, 2), lax.div(src, 2)].astype(F32)
        outs[3].start()

    def compute(s):
        for k in steps[s]:
            mirror = 0 if s == 0 else 4 if s == 4 else k + 4 if k < 4 else k - 4
            for other in (False, True):
                if k or other:
                    sib_in(mirror, other).wait_recv()
                ff = piece(k, c, other)
                at = pl.ds(pl.multiple_of(ff * 512, 512), 512)
                w = W[ff].reshape(512, 512)
                keysf[...] += dot(normed[:, at], w, 1, 0)
                b = dot(kg[...], w, 1, 1)
                back[:, at] = b
                v = b * (tok[:, at].astype(F32) * wide(rstd[...]))
                dots[...] += (v[:, :128] + v[:, 128:256]) + (v[:, 256:384] + v[:, 384:])

    def final():
        keysb[...] = keysf[...].astype(BF16)
        outs[6].start()
        mean = jnp.sum(dots[...], axis=1, keepdims=True) * (1.0 / 8192)
        dots[...] = jnp.broadcast_to(mean, dots.shape)

        @pl.loop(0, 16)
        def _(i):
            at = pl.ds(pl.multiple_of(i * 512, 512), 512)
            r = wide(rstd[...])
            hat = tok[:, at].astype(F32) * r
            tok[:, at] = (r * (back[:, at] - hat * wide(dots[...]))).astype(BF16)

        for i in range(8):
            ig_out(i).start()

    run = dict(send0=send0, update=update, spread=spread, final=final)
    for s in range(5):
        run[f"ag{s}"] = functools.partial(gather, s)
        run[f"agy{s}"] = functools.partial(gather_y, s)
        run[f"comp{s}"] = functools.partial(compute, s)
    for g in range(4):
        run[f"prod{g}"] = functools.partial(product, g)
        run[f"pair{g}"] = functools.partial(pair_sum, g)
        run[f"xb{g}"] = functools.partial(x_second, g)
        run[f"y{g}"] = functools.partial(y_stage, g)
        run[f"z{g}"] = functools.partial(z_stage, g)
    for name in ORDER:
        run[name]()

    for copy in sent:
        copy.wait_send()
    for g in range(4):
        for i in range(2):

            @pl.when(z != 2 * g + i)
            def _():
                zsend(g, i).wait_send()

    for copy in outs:
        copy.wait()
    for i in range(8):
        ig_out(i).wait()


def on_device(tokens, key_grad, weight, master, moment_one, moment_two, live, buddy):
    hbm = pl.BlockSpec(memory_space=pl.ANY)
    dma = pltpu.SemaphoreType.DMA
    out = jax.ShapeDtypeStruct
    vm = pltpu.VMEM
    keys, ig, nw, nm, n1, n2, held = pl.pallas_call(
        kernel,
        out_shape=(
            out((256, 512), BF16),
            out((256, 8192), BF16),
            out((8, 2, 32, 512), BF16),
            out((32, 512), F32),
            out((32, 512), F32),
            out((32, 512), F32),
            out((3, 32, 512), F32),
        ),
        in_specs=[hbm] * 6
        + [pl.BlockSpec(memory_space=pltpu.VMEM), pl.BlockSpec(memory_space=pltpu.SMEM)],
        out_specs=(hbm,) * 7,
        scratch_shapes=[
            vm((256, 8192), BF16),
            vm((256, 512), BF16),
            vm((256, 512), BF16),
            vm((16, 2, 2, 128, 512), BF16),
            vm((256, 8192), F32),
            vm((256, 512), F32),
            vm((256, 512), BF16),
            vm((256, 8192), BF16),
            vm((256, 128), F32),
            vm((256, 128), F32),
            vm((4, 2, 4, 2, 4, 32, 512), BF16),
            vm((4, 4, 2, 4, 32, 512), BF16),
            vm((4, 4, 4, 32, 512), BF16),
            vm((4, 2, 4, 32, 512), BF16),
            vm((4, 4, 2, 32, 512), BF16),
            vm((4, 3, 2, 32, 512), BF16),
            vm((4, 2, 32, 512), BF16),
            vm((8, 32, 512), BF16),
            vm((32, 512), F32),
            vm((2, 8, 3, 32, 512), BF16),
            vm((3, 32, 512), F32),
            vm((3, 32, 512), F32),
            vm((3, 32, 512), F32),
            dma((16,)),
            dma((4,)), dma((4,)),
            dma((4, 4)), dma((4, 4)),
            dma((4, 2)), dma((4, 2)),
            dma((4, 3)), dma((4, 3)),
            dma((4, 2)), dma((8,)),
            dma((7,)), dma((7,)),
            dma((8, 2)), dma((8, 2)),
            dma((16,)), dma((16,)),
            dma((7,)), dma((7,)),
            dma((1,)), dma((1,)),
        ],
        compiler_params=pltpu.CompilerParams(
            collective_id=0, has_side_effects=True, vmem_limit_bytes=58 << 20
        ),
        cost_estimate=pl.CostEstimate(flops=6 << 30, bytes_accessed=24 << 20, transcendentals=0),
    )(tokens, key_grad, weight.reshape(2, 2, 128, 512), master, moment_one, moment_two, live, buddy)
    return keys, ig, nw.reshape(512, 512), nm, n1, n2, held


def solution(mesh):
    both = P(("fsdp", "dom"), None)
    return jax.shard_map(
        on_device,
        mesh=mesh,
        in_specs=(both, both, P("fsdp", None), both, both, both, P(), P()),
        out_specs=(both, both, P("fsdp", None), both, both, both, P(None, ("fsdp", "dom"), None)),
        check_vma=False,
    )
```

```python
import functools

import jax
import jax.numpy as jnp
from jax import lax
from jax.experimental import pallas as pl
from jax.experimental.pallas import tpu as pltpu
from jax.sharding import PartitionSpec as P

STEP = 100
F32 = jnp.float32
BF16 = jnp.bfloat16
MESH = pl.DeviceIdType.MESH
FIRST = "xxxxxxxx"
ORDER = (
    "prod0", "xa0", "xa1", "prod1", "xb0", "xa2", "ag1", "prod2", "xb1", "xa3", "y0", "agy0",
    "c0", "xb2", "xa4", "y1", "ag2", "agy1", "c1", "prod3", "xb3", "xa5", "y2", "z0", "c2",
    "xb4", "xa6", "y3", "z1", "ag3", "agy2", "c3", "xb5", "xa7", "y4", "z2", "c4", "xb6", "y5",
    "z3", "ag4", "agy3", "c5", "xb7", "y6", "z4", "c6", "c7", "y7", "z5", "agy4", "z6", "z7",
    "update", "c8", "c9", "c10", "c11", "c12", "c13", "c14", "c15", "final", "spread",
)


def dot(a, b, ca, cb):
    return lax.dot_general(a, b, (((ca,), (cb,)), ((), ())), preferred_element_type=F32)


def kernel(
    tok_h, kg_h, w_h, ma_h, mo_h, mt_h, live_v, buddy_s,
    keys_o, ig_o, nw_o, nm_o, n1_o, n2_o, held_o,
    tok, tokS, kg, kgs, W, back, keysf, rstd, dots, Q, XA, XB, YS, YR, ZS, ZR, GA,
    state,
    loc, tk_s, tk_r, kg_s, kg_r, xa_s, xa_r, xb_s, xb_r, ys_s, ys_r, zs_s, zs_r,
    az_s, az_r, ay_s, ay_r, sib_s, sib_r, ga_s, ga_r, gs_s, gs_r,
):
    f = lax.axis_index("fsdp")
    d = lax.axis_index("dom")
    z, ylo = lax.div(f, 2), lax.rem(f, 2)
    yhi, x, c = lax.div(d, 8), lax.rem(lax.div(d, 2), 4), lax.rem(d, 2)
    y = yhi * 2 + ylo
    o = 1 - c

    def dev(x, y, z, c):
        return (z * 2 + lax.rem(y, 2), lax.div(y, 2) * 8 + x * 2 + c)

    def xat(j):
        return lax.rem(x + j, 4)

    def yat(j):
        return lax.rem(y + j, 4)

    def zat(j):
        return lax.rem(z + j, 8)

    sibling = dev(x, y, z, o)

    def local(i, src, dst):
        return pltpu.make_async_copy(src, dst, loc.at[i])

    def remote(src, dst, s, r, to):
        return pltpu.make_async_remote_copy(
            src_ref=src, dst_ref=dst, send_sem=s, recv_sem=r, device_id=to, device_id_type=MESH
        )

    sent = []

    def go(copy):
        copy.start()
        sent.append(copy)

    barrier = pltpu.get_barrier_semaphore()
    partners = [sibling]
    partners += [dev(xat(i), y, z, c) for i in (1, 2, 3)]
    partners += [dev(xat(i), yat(2), z, c) for i in (0, 1, 2, 3)]
    partners += [dev(x, yat(i), z, c) for i in (1, 3)]
    partners += [dev(x, y, zat(i), cc) for i in range(1, 8) for cc in range(2)]
    for who in partners:
        pl.semaphore_signal(barrier, inc=1, device_id=who, device_id_type=MESH)

    loads = [
        local(0, w_h, W.at[f]),
        local(1, tok_h, tok),
        local(2, kg_h, kg),
        local(3, ma_h, state.at[0]),
        local(4, mo_h, state.at[1]),
        local(5, mt_h, state.at[2]),
    ]
    for i in (1, 2, 0, 3, 4, 5):
        loads[i].start()

    def z_offset(k, core):
        one = 1 - 2 * core
        return -one * k if k <= 4 else one * (k - 4)

    def piece(k, core, other):
        zz = lax.rem(z + z_offset(k, core) + 8, 8)
        return zz * 2 + (1 - ylo if other else ylo)

    onward = dev(x, y, lax.rem(z + 1 - 2 * c + 8, 8), c)
    backward = dev(x, y, lax.rem(z - 1 + 2 * c + 8, 8), c)

    def az(k):
        to = onward if k < 5 else backward
        before = (k - 1) if k != 5 else 0
        src = W.at[piece(before, c, False), c]
        return remote(src, src, az_s.at[k - 1], az_r.at[k - 1], to)

    def az_in(k):
        src = W.at[piece(k, c, False), c]
        return remote(src, src, az_s.at[k - 1], az_r.at[k - 1], onward)

    def ay(k, side):
        src = W.at[piece(k, c, False), c, side]
        return remote(src, src, ay_s.at[k, side], ay_r.at[k, side], dev(x, yat(1 if side == 0 else 3), z, c))

    def ay_in(k, side):
        src = W.at[piece(k, c, True), c, side]
        return remote(src, src, ay_s.at[k, side], ay_r.at[k, side], dev(x, yat(1), z, c))

    def sib(k, other):
        src = W.at[piece(k, c, other), c]
        i = k + 8 * other
        return remote(src, src, sib_s.at[i], sib_r.at[i], sibling)

    def sib_in(k, other):
        src = W.at[piece(k, o, other), o]
        i = k + 8 * other
        return remote(src, src, sib_s.at[i], sib_r.at[i], sibling)

    steps = {0: (0,), 1: (1, 5), 2: (2, 6), 3: (3, 7), 4: (4,)}

    def gather(s):
        for k in steps[s]:
            if s:
                az_in(k).wait_recv()
            if k == 0:
                go(az(1))
                go(az(5))
            elif k not in (4, 7):
                go(az(k + 1))
            go(ay(k, 0))
            go(ay(k, 1))
            if k:
                go(sib(k, False))

    def gather_y(s):
        for k in steps[s]:
            ay_in(k, 0).wait_recv()
            ay_in(k, 1).wait_recv()
            go(sib(k, True))

    def wide(column):
        return jnp.concatenate([column] * 4, axis=1)

    def folded(v):
        return (v[:, :128] + v[:, 128:256]) + (v[:, 256:384] + v[:, 384:])

    def block(i):
        return pl.ds(pl.multiple_of(i * 512, 512), 512)

    loads[1].wait()
    dots[...] = jnp.zeros_like(dots)

    @pl.loop(0, 16)
    def _(i):
        v = tok[:, block(i)].astype(F32)
        dots[...] += folded(v * v)

    mean_square = jnp.sum(dots[...], axis=1, keepdims=True) * (1.0 / 8192)
    rstd[...] = jnp.broadcast_to(lax.rsqrt(mean_square + 1e-05), rstd.shape)
    dots[...] = jnp.zeros_like(dots)
    keysf[...] = jnp.zeros_like(keysf)
    flags = live_v[...].astype(F32)
    rows = lax.broadcasted_iota(jnp.int32, flags.shape, 0)
    cols = lax.broadcasted_iota(jnp.int32, flags.shape, 1)
    alive = jnp.sum(jnp.where((rows == f) & (cols == d), flags, 0.0))
    loads[2].wait()
    kgs[c] = (kg[...].astype(F32) * (wide(rstd[...]) * alive)).astype(BF16)

    pl.semaphore_wait(barrier, len(partners))

    def tokens_out(g):
        src = tok.at[:, pl.ds(pl.multiple_of((4 * o + g) * 1024, 1024), 1024)]
        return remote(src, tokS.at[g], tk_s.at[g], tk_r.at[g], sibling)

    def kg_out(core):
        return remote(kgs.at[core], kgs.at[core], kg_s.at[0], kg_r.at[0], sibling)

    go(kg_out(c))
    for g in range(4):
        go(tokens_out(g))
    loads[0].wait()
    gather(0)

    def product(g):
        if g == 0:
            kg_out(o).wait_recv()
        tokens_out(g).wait_recv()

        @pl.loop(0, 2)
        def _(low):
            mine = tok[:, block((4 * c + g) * 2 + low)]
            theirs = tokS[g, :, block(low)]
            part = (dot(mine, kgs[c], 0, 0) + dot(theirs, kgs[o], 0, 0)).astype(BF16)
            for yy in range(2):
                for xx in range(4):
                    for h in range(2):
                        row = yy * 256 + xx * 64 + h * 32
                        n = 2 * g + h
                        if FIRST[n] == "x":
                            Q[n, xx, 2 * yy + low] = part[row : row + 32]
                        else:
                            Q[n, 2 * yy + low, xx] = part[row : row + 32]

    def at_a(n, j):
        return xat(j) if FIRST[n] == "x" else yat(j)

    def at_b(n, j):
        return yat(j) if FIRST[n] == "x" else xat(j)

    def to_a(n, j):
        return dev(xat(j), y, z, c) if FIRST[n] == "x" else dev(x, yat(j), z, c)

    def to_b(n, j):
        return dev(x, yat(j), z, c) if FIRST[n] == "x" else dev(xat(j), y, z, c)

    def xa(n, i):
        j, h, to = ((2, 0, 1), (1, 1, 1), (2, 1, 3), (3, 0, 3))[i]
        src = Q.at[n, at_a(n, j), pl.ds(2 * h, 2)]
        return remote(src, XA.at[n, i], xa_s.at[n, i], xa_r.at[n, i], to_a(n, to))

    def xb(n, i):
        j = (1, 3)[i]
        src = Q.at[n, at_a(n, j), pl.ds(2 * i, 2)]
        return remote(src, XB.at[n, i], xb_s.at[n, i], xb_r.at[n, i], to_a(n, j))

    def x_first(n):
        for i in (0, 2, 1, 3):
            go(xa(n, i))

    def x_second(n):
        for i, j in ((0, 1), (1, 3)):
            xa(n, 2 * i).wait_recv()
            at = at_a(n, j)
            for b in range(2):
                Q[n, at, 2 * i + b] = (
                    Q[n, at, 2 * i + b].astype(F32) + XA[n, 2 * i, b].astype(F32)
                ).astype(BF16)
            go(xb(n, i))

    def ysend(n, j):
        return remote(
            YS.at[n, at_b(n, j)], YR.at[n, j - 1], ys_s.at[n, j - 1], ys_r.at[n, j - 1], to_b(n, j)
        )

    def y_stage(n):
        here = at_a(n, 0)
        for h, i in ((0, 3), (1, 1)):
            xa(n, i).wait_recv()
            xb(n, h).wait_recv()
            for b in range(2):
                total = Q[n, here, 2 * h + b].astype(F32) + XA[n, i, b].astype(F32)
                YS[n, 2 * h + b] = (total + XB[n, h, b].astype(F32)).astype(BF16)
        for j in (2, 1, 3):
            go(ysend(n, j))

    def zsend(n):
        return remote(
            ZS.at[n], ZR.at[z], zs_s.at[n], zs_r.at[z], dev(x, y, 4 * c + n // 2, n % 2)
        )

    def kept(n):
        return (z == 4 * c + n // 2) & (c == n % 2)

    def z_stage(n):
        total = YS[n, at_b(n, 0)].astype(F32)
        for j in (1, 2, 3):
            ysend(n, j).wait_recv()
            total = total + YR[n, j - 1].astype(F32)

        @pl.when(kept(n))
        def _():
            ZR[z] = total.astype(BF16)

        @pl.when(jnp.logical_not(kept(n)))
        def _():
            ZS[n] = total.astype(BF16)
            zsend(n).start()

    chip = lax.div(d, 2)
    others = [(i, j) for j in (0, 2) for i in range(4) if i or j]

    def spread_out(n):
        i, j = others[n]
        return remote(GA.at[c, chip], GA.at[c, chip], ga_s.at[n], ga_r.at[n], dev(xat(i), yat(j), z, c))

    def source(n):
        i, j = others[n]
        return lax.div(yat(j), 2) * 4 + lax.rem(x - i + 4, 4)

    def spread_in(n):
        slot = GA.at[c, source(n)]
        return remote(slot, slot, ga_s.at[n], ga_r.at[n], sibling)

    def relay(n, core):
        slot = GA.at[core, source(n) if n < 7 else chip]
        return remote(slot, slot, gs_s.at[n], gs_r.at[n], sibling)

    def update():
        total = jnp.zeros((32, 512), F32)
        for j in range(1, 9):
            slot = zat(j)
            here = ZR.at[slot]
            if j < 8:
                remote(here, here, zs_s.at[0], zs_r.at[slot], sibling).wait_recv()
            else:

                @pl.when(c != lax.div(z, 4))
                def _():
                    remote(here, here, zs_s.at[0], zs_r.at[slot], sibling).wait_recv()

            total = total + ZR[slot].astype(F32)
        grad = total * (256.0 / (jnp.sum(live_v[...].astype(F32)) * 256.0))
        for copy in loads[3:]:
            copy.wait()
        one = 0.9 * state[1] + 0.1 * grad
        two = 0.95 * state[2] + 0.05 * grad * grad
        first = 1.0 - 0.9**STEP
        second = 1.0 - 0.95**STEP
        step = one / first / (jnp.sqrt(two / second) + 1e-08)
        master = state[0] - 0.002 * (step + 0.1 * state[0])
        for i, (v, ref) in enumerate(((master, nm_o), (one, n1_o), (two, n2_o))):
            ref[...] = v
            GA[c, chip, i] = v.astype(BF16)
        for n in range(7):
            go(spread_out(n))
        go(relay(7, c))

    def spread():
        for n in range(7):
            spread_in(n).wait_recv()
            go(relay(n, c))
        for n in range(8):
            relay(n, o).wait_recv()
        for core in range(2):
            nw_o[:, core] = GA[core, :, 0]
        src = jnp.int32(0)
        for s in range(16):
            src = jnp.where(buddy_s[s] == d, s, src)
        held_o[...] = GA[lax.rem(src, 2), lax.div(src, 2)].astype(F32)

    tasks = [(s, k, other) for s in range(5) for other in (False, True) for k in steps[s]]

    def compute(i):
        s, k, other = tasks[i]
        mirror = 0 if s == 0 else 4 if s == 4 else k + 4 if k < 4 else k - 4
        if k or other:
            sib_in(mirror, other).wait_recv()
        ff = piece(k, c, other)
        w = W[ff].reshape(512, 512)
        t = tok[:, block(ff)].astype(F32)
        keysf[...] += dot((t * wide(rstd[...])).astype(BF16), w, 1, 0)
        b = dot(kg[...], w, 1, 1)
        back[:, block(ff)] = b
        dots[...] += folded(b * t)

    def final():
        r = rstd[...]
        keys_o[...] = keysf[...].astype(BF16)
        mean = jnp.sum(dots[...], axis=1, keepdims=True) * (1.0 / 8192)
        dots[...] = r * r * r * mean

        @pl.loop(0, 16)
        def _(i):
            at = block(i)
            less = tok[:, at].astype(F32) * wide(dots[...])
            ig_o[:, at] = (wide(rstd[...]) * back[:, at] - less).astype(BF16)

    run = dict(update=update, spread=spread, final=final)
    for s in range(5):
        run[f"ag{s}"] = functools.partial(gather, s)
        run[f"agy{s}"] = functools.partial(gather_y, s)
    for i in range(16):
        run[f"c{i}"] = functools.partial(compute, i)
    for g in range(4):
        run[f"prod{g}"] = functools.partial(product, g)
    for n in range(8):
        run[f"xa{n}"] = functools.partial(x_first, n)
        run[f"xb{n}"] = functools.partial(x_second, n)
        run[f"y{n}"] = functools.partial(y_stage, n)
        run[f"z{n}"] = functools.partial(z_stage, n)
    for name in ORDER:
        run[name]()

    for copy in sent:
        copy.wait_send()
    for n in range(8):

        @pl.when(jnp.logical_not(kept(n)))
        def _():
            zsend(n).wait_send()


def hand_on(*refs):
    n = len(refs) // 2
    copies = [pltpu.make_async_copy(refs[i], refs[n + i], refs[-1].at[i]) for i in range(n)]
    for copy in copies:
        copy.start()
    for copy in copies:
        copy.wait()


def on_device(tokens, key_grad, weight, master, moment_one, moment_two, live, buddy):
    hbm = pl.BlockSpec(memory_space=pl.ANY)
    dma = pltpu.SemaphoreType.DMA
    out = jax.ShapeDtypeStruct
    vm = pltpu.VMEM
    shapes = (
        out((256, 512), BF16),
        out((256, 8192), BF16),
        out((8, 2, 32, 512), BF16),
        out((32, 512), F32),
        out((32, 512), F32),
        out((32, 512), F32),
        out((3, 32, 512), F32),
    )
    made = pl.pallas_call(
        kernel,
        out_shape=tuple(pltpu.VMEM(one.shape, one.dtype) for one in shapes),
        in_specs=[hbm] * 6
        + [pl.BlockSpec(memory_space=pltpu.VMEM), pl.BlockSpec(memory_space=pltpu.SMEM)],
        out_specs=(pl.BlockSpec(memory_space=pltpu.VMEM),) * 7,
        scratch_shapes=[
            vm((256, 8192), BF16),
            vm((4, 256, 1024), BF16),
            vm((256, 512), BF16),
            vm((2, 256, 512), BF16),
            vm((16, 2, 2, 128, 512), BF16),
            vm((256, 8192), F32),
            vm((256, 512), F32),
            vm((256, 128), F32),
            vm((256, 128), F32),
            vm((8, 4, 4, 32, 512), BF16),
            vm((8, 4, 2, 32, 512), BF16),
            vm((8, 2, 2, 32, 512), BF16),
            vm((8, 4, 32, 512), BF16),
            vm((8, 3, 32, 512), BF16),
            vm((8, 32, 512), BF16),
            vm((8, 32, 512), BF16),
            vm((2, 8, 3, 32, 512), BF16),
            vm((3, 32, 512), F32),
            dma((6,)),
            dma((4,)), dma((4,)),
            dma((1,)), dma((1,)),
            dma((8, 4)), dma((8, 4)),
            dma((8, 2)), dma((8, 2)),
            dma((8, 3)), dma((8, 3)),
            dma((8,)), dma((8,)),
            dma((7,)), dma((7,)),
            dma((8, 2)), dma((8, 2)),
            dma((16,)), dma((16,)),
            dma((7,)), dma((7,)),
            dma((8,)), dma((8,)),
        ],
        compiler_params=pltpu.CompilerParams(
            collective_id=0, has_side_effects=True, vmem_limit_bytes=58 << 20
        ),
        cost_estimate=pl.CostEstimate(flops=6 << 30, bytes_accessed=24 << 20, transcendentals=0),
    )(tokens, key_grad, weight.reshape(2, 2, 128, 512), master, moment_one, moment_two, live, buddy)
    made = [pltpu.with_memory_space_constraint(one, pltpu.VMEM) for one in made]
    keys, ig, nw, nm, n1, n2, held = pl.pallas_call(
        hand_on,
        out_shape=shapes,
        in_specs=[pl.BlockSpec(memory_space=pltpu.VMEM)] * 7,
        out_specs=(hbm,) * 7,
        scratch_shapes=[dma((7,))],
        compiler_params=pltpu.CompilerParams(vmem_limit_bytes=4 << 20),
    )(*made)
    return keys, ig, nw.reshape(512, 512), nm, n1, n2, held


def solution(mesh):
    both = P(("fsdp", "dom"), None)
    return jax.shard_map(
        on_device,
        mesh=mesh,
        in_specs=(both, both, P("fsdp", None), both, both, both, P(), P()),
        out_specs=(both, both, P("fsdp", None), both, both, both, P(None, ("fsdp", "dom"), None)),
        check_vma=False,
    )
```

```python
import functools

import jax
import jax.numpy as jnp
from jax import lax
from jax.experimental import pallas as pl
from jax.experimental.pallas import tpu as pltpu
from jax.sharding import PartitionSpec as P

STEP = 100
F32 = jnp.float32
BF16 = jnp.bfloat16
MESH = pl.DeviceIdType.MESH
FIRST = "yxxxxxxx"
ORDER = (
    "prod0", "xa0", "xa1", "prod1", "xb0", "xa2", "ag1", "prod2", "xb1", "xa3", "y0", "agy0",
    "c0", "xb2", "xa4", "y1", "ag2", "agy1", "c1", "prod3", "xb3", "xa5", "y2", "z0", "c2",
    "xb4", "xa6", "y3", "z1", "ag3", "agy2", "c3", "xb5", "xa7", "y4", "z2", "c4", "xb6", "y5",
    "z3", "ag4", "agy3", "c5", "xb7", "y6", "z4", "c6", "c7", "y7", "z5", "agy4", "z6", "z7",
    "update", "c8", "c9", "c10", "c11", "c12", "c13", "c14", "c15", "final", "spread",
)


def dot(a, b, ca, cb):
    return lax.dot_general(a, b, (((ca,), (cb,)), ((), ())), preferred_element_type=F32)


def kernel(
    tok_h, kg_h, w_h, ma_h, mo_h, mt_h, live_v, buddy_s,
    keys_o, ig_o, nw_o, nm_o, n1_o, n2_o, held_o,
    tok, tokS, kg, kgs, W, back, keysf, rstd, dots, Q, XA, XB, YS, YR, ZS, ZR, GA,
    state,
    loc, tk_s, tk_r, kg_s, kg_r, xa_s, xa_r, xb_s, xb_r, ys_s, ys_r, zs_s, zs_r,
    az_s, az_r, ay_s, ay_r, sib_s, sib_r, ga_s, ga_r, gs_s, gs_r,
):
    f = lax.axis_index("fsdp")
    d = lax.axis_index("dom")
    z, ylo = lax.div(f, 2), lax.rem(f, 2)
    yhi, x, c = lax.div(d, 8), lax.rem(lax.div(d, 2), 4), lax.rem(d, 2)
    y = yhi * 2 + ylo
    o = 1 - c

    def dev(x, y, z, c):
        return (z * 2 + lax.rem(y, 2), lax.div(y, 2) * 8 + x * 2 + c)

    def xat(j):
        return lax.rem(x + j, 4)

    def yat(j):
        return lax.rem(y + j, 4)

    def zat(j):
        return lax.rem(z + j, 8)

    sibling = dev(x, y, z, o)

    def local(i, src, dst):
        return pltpu.make_async_copy(src, dst, loc.at[i])

    def remote(src, dst, s, r, to):
        return pltpu.make_async_remote_copy(
            src_ref=src, dst_ref=dst, send_sem=s, recv_sem=r, device_id=to, device_id_type=MESH
        )

    sent = []

    def go(copy):
        copy.start()
        sent.append(copy)

    def quarter(i):
        at = pl.ds(i * 2048, 2048)
        return local(6 + i, tok_h.at[:, at], tok.at[:, at])

    for i in range(4):
        quarter(i).start()
    loads = [
        local(0, w_h, W.at[f]),
        local(1, kg_h, kg),
        local(2, ma_h, state.at[0]),
        local(3, mo_h, state.at[1]),
        local(4, mt_h, state.at[2]),
    ]
    for i in (1, 0, 2, 3, 4):
        loads[i].start()

    barrier = pltpu.get_barrier_semaphore()
    partners = [sibling]
    partners += [dev(xat(i), y, z, c) for i in (1, 2, 3)]
    partners += [dev(xat(i), yat(2), z, c) for i in (0, 1, 2, 3)]
    partners += [dev(x, yat(i), z, c) for i in (1, 3)]
    partners += [dev(x, y, zat(i), cc) for i in range(1, 8) for cc in range(2)]
    for who in partners:
        pl.semaphore_signal(barrier, inc=1, device_id=who, device_id_type=MESH)

    def z_offset(k, core):
        one = 1 - 2 * core
        return -one * k if k <= 4 else one * (k - 4)

    def piece(k, core, other):
        zz = lax.rem(z + z_offset(k, core) + 8, 8)
        return zz * 2 + (1 - ylo if other else ylo)

    onward = dev(x, y, lax.rem(z + 1 - 2 * c + 8, 8), c)
    backward = dev(x, y, lax.rem(z - 1 + 2 * c + 8, 8), c)

    def az(k):
        to = onward if k < 5 else backward
        before = (k - 1) if k != 5 else 0
        src = W.at[piece(before, c, False), c]
        return remote(src, src, az_s.at[k - 1], az_r.at[k - 1], to)

    def az_in(k):
        src = W.at[piece(k, c, False), c]
        return remote(src, src, az_s.at[k - 1], az_r.at[k - 1], onward)

    def ay(k, side):
        src = W.at[piece(k, c, False), c, side]
        return remote(src, src, ay_s.at[k, side], ay_r.at[k, side], dev(x, yat(1 if side == 0 else 3), z, c))

    def ay_in(k, side):
        src = W.at[piece(k, c, True), c, side]
        return remote(src, src, ay_s.at[k, side], ay_r.at[k, side], dev(x, yat(1), z, c))

    def sib(k, other):
        src = W.at[piece(k, c, other), c]
        i = k + 8 * other
        return remote(src, src, sib_s.at[i], sib_r.at[i], sibling)

    def sib_in(k, other):
        src = W.at[piece(k, o, other), o]
        i = k + 8 * other
        return remote(src, src, sib_s.at[i], sib_r.at[i], sibling)

    steps = {0: (0,), 1: (1, 5), 2: (2, 6), 3: (3, 7), 4: (4,)}

    def gather(s):
        for k in steps[s]:
            if s:
                az_in(k).wait_recv()
            if k == 0:
                go(az(1))
                go(az(5))
            elif k not in (4, 7):
                go(az(k + 1))
            go(ay(k, 0))
            go(ay(k, 1))
            if k:
                go(sib(k, False))

    def gather_y(s):
        for k in steps[s]:
            ay_in(k, 0).wait_recv()
            ay_in(k, 1).wait_recv()
            go(sib(k, True))

    def wide(column):
        return jnp.concatenate([column] * 4, axis=1)

    def folded(v):
        return (v[:, :128] + v[:, 128:256]) + (v[:, 256:384] + v[:, 384:])

    def block(i):
        return pl.ds(pl.multiple_of(i * 512, 512), 512)

    dots[...] = jnp.zeros_like(dots)
    for part in range(4):
        quarter(part).wait()

        @pl.loop(4 * part, 4 * part + 4)
        def _(i):
            v = tok[:, block(i)].astype(F32)
            dots[...] += folded(v * v)

    mean_square = jnp.sum(dots[...], axis=1, keepdims=True) * (1.0 / 8192)
    rstd[...] = jnp.broadcast_to(lax.rsqrt(mean_square + 1e-05), rstd.shape)
    dots[...] = jnp.zeros_like(dots)
    keysf[...] = jnp.zeros_like(keysf)
    flags = live_v[...].astype(F32)
    rows = lax.broadcasted_iota(jnp.int32, flags.shape, 0)
    cols = lax.broadcasted_iota(jnp.int32, flags.shape, 1)
    alive = jnp.sum(jnp.where((rows == f) & (cols == d), flags, 0.0))
    loads[1].wait()
    kgs[c] = (kg[...].astype(F32) * (wide(rstd[...]) * alive)).astype(BF16)

    pl.semaphore_wait(barrier, len(partners))

    def tokens_out(g):
        src = tok.at[:, pl.ds(pl.multiple_of((4 * o + g) * 1024, 1024), 1024)]
        return remote(src, tokS.at[g], tk_s.at[g], tk_r.at[g], sibling)

    def kg_out(core):
        return remote(kgs.at[core], kgs.at[core], kg_s.at[0], kg_r.at[0], sibling)

    go(kg_out(c))
    for g in range(4):
        go(tokens_out(g))
    loads[0].wait()
    gather(0)

    def product(g):
        if g == 0:
            kg_out(o).wait_recv()
        tokens_out(g).wait_recv()

        @pl.loop(0, 2)
        def _(low):
            mine = tok[:, block((4 * c + g) * 2 + low)]
            theirs = tokS[g, :, block(low)]
            part = (dot(mine, kgs[c], 0, 0) + dot(theirs, kgs[o], 0, 0)).astype(BF16)
            for yy in range(2):
                for xx in range(4):
                    for h in range(2):
                        row = yy * 256 + xx * 64 + h * 32
                        n = 2 * g + h
                        if FIRST[n] == "x":
                            Q[n, xx, 2 * yy + low] = part[row : row + 32]
                        else:
                            Q[n, 2 * yy + low, xx] = part[row : row + 32]

    def at_a(n, j):
        return xat(j) if FIRST[n] == "x" else yat(j)

    def at_b(n, j):
        return yat(j) if FIRST[n] == "x" else xat(j)

    def to_a(n, j):
        return dev(xat(j), y, z, c) if FIRST[n] == "x" else dev(x, yat(j), z, c)

    def to_b(n, j):
        return dev(x, yat(j), z, c) if FIRST[n] == "x" else dev(xat(j), y, z, c)

    def xa(n, i):
        j, h, to = ((2, 0, 1), (1, 1, 1), (2, 1, 3), (3, 0, 3))[i]
        src = Q.at[n, at_a(n, j), pl.ds(2 * h, 2)]
        return remote(src, XA.at[n, i], xa_s.at[n, i], xa_r.at[n, i], to_a(n, to))

    def xb(n, i):
        j = (1, 3)[i]
        src = Q.at[n, at_a(n, j), pl.ds(2 * i, 2)]
        return remote(src, XB.at[n, i], xb_s.at[n, i], xb_r.at[n, i], to_a(n, j))

    def x_first(n):
        for i in (0, 2, 1, 3):
            go(xa(n, i))

    def x_second(n):
        for i, j in ((0, 1), (1, 3)):
            xa(n, 2 * i).wait_recv()
            at = at_a(n, j)
            for b in range(2):
                Q[n, at, 2 * i + b] = (
                    Q[n, at, 2 * i + b].astype(F32) + XA[n, 2 * i, b].astype(F32)
                ).astype(BF16)
            go(xb(n, i))

    def ysend(n, j):
        return remote(
            YS.at[n, at_b(n, j)], YR.at[n, j - 1], ys_s.at[n, j - 1], ys_r.at[n, j - 1], to_b(n, j)
        )

    def y_stage(n):
        here = at_a(n, 0)
        for h, i in ((0, 3), (1, 1)):
            xa(n, i).wait_recv()
            xb(n, h).wait_recv()
            for b in range(2):
                total = Q[n, here, 2 * h + b].astype(F32) + XA[n, i, b].astype(F32)
                YS[n, 2 * h + b] = (total + XB[n, h, b].astype(F32)).astype(BF16)
        for j in (2, 1, 3):
            go(ysend(n, j))

    def zsend(n):
        return remote(
            ZS.at[n], ZR.at[z], zs_s.at[n], zs_r.at[z], dev(x, y, 4 * c + n // 2, n % 2)
        )

    def kept(n):
        return (z == 4 * c + n // 2) & (c == n % 2)

    def z_stage(n):
        total = YS[n, at_b(n, 0)].astype(F32)
        for j in (1, 2, 3):
            ysend(n, j).wait_recv()
            total = total + YR[n, j - 1].astype(F32)

        @pl.when(kept(n))
        def _():
            ZR[z] = total.astype(BF16)

        @pl.when(jnp.logical_not(kept(n)))
        def _():
            ZS[n] = total.astype(BF16)
            zsend(n).start()

    chip = lax.div(d, 2)
    others = [(i, j) for j in (0, 2) for i in range(4) if i or j]

    def spread_out(n):
        i, j = others[n]
        return remote(GA.at[c, chip], GA.at[c, chip], ga_s.at[n], ga_r.at[n], dev(xat(i), yat(j), z, c))

    def source(n):
        i, j = others[n]
        return lax.div(yat(j), 2) * 4 + lax.rem(x - i + 4, 4)

    def spread_in(n):
        slot = GA.at[c, source(n)]
        return remote(slot, slot, ga_s.at[n], ga_r.at[n], sibling)

    def relay(n, core):
        slot = GA.at[core, source(n) if n < 7 else chip]
        return remote(slot, slot, gs_s.at[n], gs_r.at[n], sibling)

    def update():
        total = jnp.zeros((32, 512), F32)
        for j in range(1, 9):
            slot = zat(j)
            here = ZR.at[slot]
            if j < 8:
                remote(here, here, zs_s.at[0], zs_r.at[slot], sibling).wait_recv()
            else:

                @pl.when(c != lax.div(z, 4))
                def _():
                    remote(here, here, zs_s.at[0], zs_r.at[slot], sibling).wait_recv()

            total = total + ZR[slot].astype(F32)
        grad = total * (256.0 / (jnp.sum(live_v[...].astype(F32)) * 256.0))
        for copy in loads[2:]:
            copy.wait()
        one = 0.9 * state[1] + 0.1 * grad
        two = 0.95 * state[2] + 0.05 * grad * grad
        first = 1.0 - 0.9**STEP
        second = 1.0 - 0.95**STEP
        step = one / first / (jnp.sqrt(two / second) + 1e-08)
        master = state[0] - 0.002 * (step + 0.1 * state[0])
        for i, (v, ref) in enumerate(((master, nm_o), (one, n1_o), (two, n2_o))):
            ref[...] = v
            GA[c, chip, i] = v.astype(BF16)
        for n in range(7):
            go(spread_out(n))
        go(relay(7, c))

    def spread():
        for n in range(7):
            spread_in(n).wait_recv()
            go(relay(n, c))
        for n in range(8):
            relay(n, o).wait_recv()
        for core in range(2):
            nw_o[:, core] = GA[core, :, 0]
        src = jnp.int32(0)
        for s in range(16):
            src = jnp.where(buddy_s[s] == d, s, src)
        held_o[...] = GA[lax.rem(src, 2), lax.div(src, 2)].astype(F32)

    tasks = [(s, k, other) for s in range(5) for other in (False, True) for k in steps[s]]

    def compute(i):
        s, k, other = tasks[i]
        mirror = 0 if s == 0 else 4 if s == 4 else k + 4 if k < 4 else k - 4
        if k or other:
            sib_in(mirror, other).wait_recv()
        ff = piece(k, c, other)
        w = W[ff].reshape(512, 512)
        t = tok[:, block(ff)].astype(F32)
        keysf[...] += dot((t * wide(rstd[...])).astype(BF16), w, 1, 0)
        b = dot(kg[...], w, 1, 1)
        back[:, block(ff)] = b
        dots[...] += folded(b * t)

    def final():
        r = rstd[...]
        keys_o[...] = keysf[...].astype(BF16)
        mean = jnp.sum(dots[...], axis=1, keepdims=True) * (1.0 / 8192)
        dots[...] = r * r * r * mean

        @pl.loop(0, 16)
        def _(i):
            at = block(i)
            less = tok[:, at].astype(F32) * wide(dots[...])
            ig_o[:, at] = (wide(rstd[...]) * back[:, at] - less).astype(BF16)

    run = dict(update=update, spread=spread, final=final)
    for s in range(5):
        run[f"ag{s}"] = functools.partial(gather, s)
        run[f"agy{s}"] = functools.partial(gather_y, s)
    for i in range(16):
        run[f"c{i}"] = functools.partial(compute, i)
    for g in range(4):
        run[f"prod{g}"] = functools.partial(product, g)
    for n in range(8):
        run[f"xa{n}"] = functools.partial(x_first, n)
        run[f"xb{n}"] = functools.partial(x_second, n)
        run[f"y{n}"] = functools.partial(y_stage, n)
        run[f"z{n}"] = functools.partial(z_stage, n)
    for name in ORDER:
        run[name]()

    for copy in sent:
        copy.wait_send()
    for n in range(8):

        @pl.when(jnp.logical_not(kept(n)))
        def _():
            zsend(n).wait_send()


def hand_on(*refs):
    n = len(refs) // 2
    copies = [pltpu.make_async_copy(refs[i], refs[n + i], refs[-1].at[i]) for i in range(n)]
    for copy in copies:
        copy.start()
    for copy in copies:
        copy.wait()


def on_device(tokens, key_grad, weight, master, moment_one, moment_two, live, buddy):
    hbm = pl.BlockSpec(memory_space=pl.ANY)
    dma = pltpu.SemaphoreType.DMA
    out = jax.ShapeDtypeStruct
    vm = pltpu.VMEM
    shapes = (
        out((256, 512), BF16),
        out((256, 8192), BF16),
        out((8, 2, 32, 512), BF16),
        out((32, 512), F32),
        out((32, 512), F32),
        out((32, 512), F32),
        out((3, 32, 512), F32),
    )
    made = pl.pallas_call(
        kernel,
        out_shape=tuple(pltpu.VMEM(one.shape, one.dtype) for one in shapes),
        in_specs=[hbm] * 6
        + [pl.BlockSpec(memory_space=pltpu.VMEM), pl.BlockSpec(memory_space=pltpu.SMEM)],
        out_specs=(pl.BlockSpec(memory_space=pltpu.VMEM),) * 7,
        scratch_shapes=[
            vm((256, 8192), BF16),
            vm((4, 256, 1024), BF16),
            vm((256, 512), BF16),
            vm((2, 256, 512), BF16),
            vm((16, 2, 2, 128, 512), BF16),
            vm((256, 8192), F32),
            vm((256, 512), F32),
            vm((256, 128), F32),
            vm((256, 128), F32),
            vm((8, 4, 4, 32, 512), BF16),
            vm((8, 4, 2, 32, 512), BF16),
            vm((8, 2, 2, 32, 512), BF16),
            vm((8, 4, 32, 512), BF16),
            vm((8, 3, 32, 512), BF16),
            vm((8, 32, 512), BF16),
            vm((8, 32, 512), BF16),
            vm((2, 8, 3, 32, 512), BF16),
            vm((3, 32, 512), F32),
            dma((10,)),
            dma((4,)), dma((4,)),
            dma((1,)), dma((1,)),
            dma((8, 4)), dma((8, 4)),
            dma((8, 2)), dma((8, 2)),
            dma((8, 3)), dma((8, 3)),
            dma((8,)), dma((8,)),
            dma((7,)), dma((7,)),
            dma((8, 2)), dma((8, 2)),
            dma((16,)), dma((16,)),
            dma((7,)), dma((7,)),
            dma((8,)), dma((8,)),
        ],
        compiler_params=pltpu.CompilerParams(
            collective_id=0, has_side_effects=True, vmem_limit_bytes=58 << 20
        ),
        cost_estimate=pl.CostEstimate(flops=6 << 30, bytes_accessed=24 << 20, transcendentals=0),
    )(tokens, key_grad, weight.reshape(2, 2, 128, 512), master, moment_one, moment_two, live, buddy)
    made = [pltpu.with_memory_space_constraint(one, pltpu.VMEM) for one in made]
    keys, ig, nw, nm, n1, n2, held = pl.pallas_call(
        hand_on,
        out_shape=shapes,
        in_specs=[pl.BlockSpec(memory_space=pltpu.VMEM)] * 7,
        out_specs=(hbm,) * 7,
        scratch_shapes=[dma((7,))],
        compiler_params=pltpu.CompilerParams(vmem_limit_bytes=4 << 20),
    )(*made)
    return keys, ig, nw.reshape(512, 512), nm, n1, n2, held


def solution(mesh):
    both = P(("fsdp", "dom"), None)
    return jax.shard_map(
        on_device,
        mesh=mesh,
        in_specs=(both, both, P("fsdp", None), both, both, both, P(), P()),
        out_specs=(both, both, P("fsdp", None), both, both, both, P(None, ("fsdp", "dom"), None)),
        check_vma=False,
    )
```
